32 devices in a mesh: section: 8 (over z, x), tensor: 4 (over y, core).
Axes of the slice: x: 2, y: 2, z: 4, core: 2. Of those that a mesh axis runs over, the one named last changes fastest.
Arguments:
- state: bfloat16 [8, 16, 2560], P('section'), may hold values from -6 to 6
- gain_in: bfloat16 [8, 2560], P('section'), may hold values from 0.25 to 1.75
- w_query: bfloat16 [8, 2560, 4096], P('section', None, 'tensor'), may hold values from -0.125 to 0.125
- w_key: bfloat16 [8, 2560, 512], P('section', None, 'tensor'), may hold values from -0.125 to 0.125
- w_value: bfloat16 [8, 2560, 512], P('section', None, 'tensor'), may hold values from -0.125 to 0.125
- w_output: bfloat16 [8, 4096, 2560], P('section', 'tensor'), may hold values from -0.375 to 0.375
- query_gain: bfloat16 [8, 128], P('section'), may hold values from 0.099609375 to 1.8984375
- key_gain: bfloat16 [8, 128], P('section'), may hold values from 0.099609375 to 1.8984375
- cache_keys: bfloat16 [8, 16, 4, 32, 128], P('section', None, 'tensor'), may hold values from -600 to 600
- cache_values: bfloat16 [8, 16, 4, 32, 128], P('section', None, 'tensor'), may hold values from -6 to 6
- lengths: int32 [8, 16], P('section'), may hold values from 4 to 32, as said below
Outputs:
- handed: bfloat16 [8, 16, 2560], P('section')
- new_keys: bfloat16 [8, 16, 4, 128], P('section', None, 'tensor')
- new_values: bfloat16 [8, 16, 4, 128], P('section', None, 'tensor')
The draws below stay inside these ranges and needn't reach their ends.
Inputs may be any that keep to these rules, and one draw needn't show every extreme that they name: `lengths`: in every section at least one row holds 32 tokens.
All inputs are finite; a program needn't handle non-finite values.
Results may differ from the reference program's by a relative error of at most 0.012.
The reference program's roundings to bfloat16 on the way count: a program that leaves them out, or rounds other values in their place, can miss the bound.
Values may be sent and summed in bfloat16 or wider, within the bound.
A program may use at most 64 MiB of HBM per device.

```python
import math
import jax
import jax.numpy as jnp
from jax import lax

D = 2560
HEADS = 32
KVH = 4
HD = 128
R = 16
CACHE = 32
SECTIONS = 8


def draw_state(key, part):
    key = jax.random.fold_in(key, 11)
    key_noise, key_rows, key_cols = jax.random.split(key, 3)
    row_scale = jnp.exp(jax.random.uniform(key_rows, (SECTIONS, R, 1), minval=math.log(0.02), maxval=math.log(0.2)))
    col_scale = jnp.exp(jax.random.uniform(key_cols, (SECTIONS, 1, D), minval=math.log(0.3), maxval=math.log(3.0)))
    noise = jax.random.normal(key_noise, (SECTIONS, R, D), dtype=jnp.float32)
    return jnp.clip(noise * row_scale * col_scale, -6.0, 6.0).astype(jnp.bfloat16)


def draw_cache_keys(key, part):
    key = jax.random.fold_in(key, 12)
    key_base = jax.random.fold_in(key, 0)
    base = jax.random.normal(key_base, (SECTIONS, R, KVH, CACHE, HD), dtype=jnp.float32)
    return jnp.clip(base, -600.0, 600.0).astype(jnp.bfloat16)


def draw_lengths(key, part):
    key = jax.random.fold_in(key, 13)
    key_base, key_pick = jax.random.split(key, 2)
    filled = jax.random.randint(key_base, (SECTIONS, R), max(1, CACHE // 8), CACHE + 1)
    chosen = jax.random.randint(key_pick, (SECTIONS, 1), 0, R)
    longest = jnp.arange(R)[None, :] == chosen
    return jnp.where(longest, CACHE, filled).astype(jnp.int32)


def level_of(own_key, shape, shards, low, largest):
    loudness, own = 1.0, jax.random.fold_in(own_key, 6)
    for axis_at, parts in shards:
        heights = jnp.exp(jax.random.uniform(jax.random.fold_in(own, axis_at), (parts,), jnp.float32, low / len(shards), largest / len(shards)))
        loudness = loudness * jnp.repeat(heights, shape[axis_at] // parts).reshape([-1 if axis == axis_at else 1 for axis in range(len(shape))])
    return loudness


def normal_values(rng, extent, width, most, cuts=(), kind=jnp.bfloat16):
    entries = jax.random.normal(rng, extent, jnp.float32) * width
    if len(cuts) > 0:
        entries = level_of(rng, extent, cuts, -0.22, 0.18) * entries
    return jnp.clip(entries, min=-most, max=most).astype(kind)


def setup_inputs(seed: int = 0) -> dict:
    seeds = jax.random.split(jax.random.key(seed), 12)
    state = draw_state(jax.random.fold_in(seeds[11], 71), 0)
    gain_in = jnp.clip(1.0 + 0.15 * jax.random.normal(seeds[1], (SECTIONS, D), jnp.float32), 0.25, 1.75).astype(jnp.bfloat16)
    w_query = normal_values(seeds[2], (SECTIONS, D, HEADS * HD), D ** -0.5, 0.125, ((0, 8), (2, 4)))
    w_key = normal_values(seeds[3], (SECTIONS, D, KVH * HD), D ** -0.5, 0.125, ((0, 8), (2, 4)))
    w_value = normal_values(seeds[4], (SECTIONS, D, KVH * HD), D ** -0.5, 0.125, ((0, 8), (2, 4)))
    w_output = normal_values(seeds[5], (SECTIONS, HEADS * HD, D), (HEADS * HD // 16) ** -0.5, 0.375, ((0, 8), (1, 4)))
    query_gain = jnp.clip(1.0 + 0.18 * jax.random.normal(seeds[6], (SECTIONS, HD), jnp.float32), 0.099609375, 1.8984375).astype(jnp.bfloat16)
    key_gain = jnp.clip(1.0 + 0.18 * jax.random.normal(seeds[7], (SECTIONS, HD), jnp.float32), 0.099609375, 1.8984375).astype(jnp.bfloat16)
    cache_keys = draw_cache_keys(jax.random.fold_in(seeds[11], 71), 0)
    cache_values = normal_values(seeds[9], (SECTIONS, R, KVH, CACHE, HD), 1.0, 6.0, ((0, 8), (2, 4)))
    lengths = draw_lengths(jax.random.fold_in(seeds[11], 71), 0)
    return dict(state=state, gain_in=gain_in, w_query=w_query, w_key=w_key, w_value=w_value, w_output=w_output, query_gain=query_gain, key_gain=key_gain, cache_keys=cache_keys, cache_values=cache_values, lengths=lengths)


epsilon = 1e-06
rope_base = 1000000.0

def rms_norm(values, gain_vec):
    return values * lax.rsqrt(lax.optimization_barrier(jnp.mean(values * values, axis=-1, keepdims=True)) + epsilon) * gain_vec.astype(jnp.float32)

def rotate(values, position):
    half_dim = values.shape[-1] // 2
    frequency = rope_base ** (-(jnp.arange(half_dim, dtype=jnp.float32) * 2.0 / values.shape[-1]))
    angles = position.astype(jnp.float32)[:, None] * frequency[None, :]
    target_shape = (angles.shape[0],) + (1,) * (values.ndim - 2) + (half_dim,)
    cosine = jnp.cos(angles).reshape(target_shape)
    sine = jnp.sin(angles).reshape(target_shape)
    lower_half = values[..., :half_dim]
    upper_half = values[..., half_dim:]
    return jnp.concatenate([lower_half * cosine - upper_half * sine, upper_half * cosine + lower_half * sine], axis=-1)

def section_tick(hidden_in, gain_in, w_query, w_key, w_value, w_output, query_gain, key_gain, cache_key, cache_val, lengths):
    row_count = hidden_in.shape[0]
    kv_heads = w_key.shape[1] // HD
    head_group = w_query.shape[1] // w_key.shape[1]
    normed = rms_norm(hidden_in.astype(jnp.float32), gain_in).astype(jnp.bfloat16)
    query = jnp.dot(normed, w_query, preferred_element_type=jnp.float32).reshape(row_count, kv_heads, head_group, HD)
    key_raw = jnp.dot(normed, w_key, preferred_element_type=jnp.float32).reshape(row_count, kv_heads, HD)
    new_value = jnp.dot(normed, w_value, preferred_element_type=jnp.float32).astype(jnp.bfloat16).reshape(row_count, kv_heads, HD)
    query_rot = rotate(rms_norm(query, query_gain), lengths).astype(jnp.bfloat16)
    new_key = rotate(rms_norm(key_raw, key_gain), lengths).astype(jnp.bfloat16)
    score_scale = HD ** (-0.5)
    cache_score = jnp.einsum('rkgd,rkjd->rkgj', query_rot.astype(jnp.float32), cache_key.astype(jnp.float32)) * score_scale
    own_score = jnp.einsum('rkgd,rkd->rkg', query_rot.astype(jnp.float32), new_key.astype(jnp.float32)) * score_scale
    in_cache = jnp.arange(cache_key.shape[2])[None, None, None, :] < lengths[:, None, None, None]
    masked = jnp.where(in_cache, cache_score, -1e+30)
    row_max = jnp.maximum(lax.optimization_barrier(jnp.max(masked, axis=-1)), own_score)
    cache_exp = jnp.where(in_cache, jnp.exp(masked - row_max[..., None]), 0.0)
    own_exp = jnp.exp(own_score - row_max)
    denom_sum = lax.optimization_barrier(jnp.sum(cache_exp, axis=-1)) + own_exp
    cache_prob = (cache_exp / denom_sum[..., None]).astype(jnp.bfloat16)
    own_prob = (own_exp / denom_sum).astype(jnp.bfloat16)
    attended = jnp.einsum('rkgj,rkjd->rkgd', cache_prob.astype(jnp.float32), cache_val.astype(jnp.float32))
    attended = attended + own_prob.astype(jnp.float32)[..., None] * new_value.astype(jnp.float32)[:, :, None, :]
    attended = attended.astype(jnp.bfloat16).reshape(row_count, kv_heads * head_group * HD)
    result = (hidden_in.astype(jnp.float32) + jnp.dot(attended, w_output, preferred_element_type=jnp.float32)).astype(jnp.bfloat16)
    return (result, new_key, new_value)

def reference(state, gain_in, w_query, w_key, w_value, w_output, query_gain, key_gain, cache_keys, cache_values, lengths):

    def per_section(section_items):
        return section_tick(*section_items)
    result, new_keys, new_values = lax.map(per_section, (state, gain_in, w_query, w_key, w_value, w_output, query_gain, key_gain, cache_keys, cache_values, lengths))
    handed = jnp.roll(result, 1, axis=0)
    return (handed, new_keys, new_values)
```

```python
import jax
import jax.numpy as jnp
from jax import lax
from jax.experimental import pallas as pl
from jax.experimental.pallas import tpu as pltpu
from jax.sharding import PartitionSpec as P

HD = 128
CORES = 2
CHUNKS = 5
EPSILON = 1e-06
ROPE_BASE = 1000000.0
MESH = pl.DeviceIdType.MESH


def inverse_rms(values):
    return lax.rsqrt(jnp.mean(values * values, axis=-1, keepdims=True) + EPSILON)


def tick_kernel(
    sections,
    tensors,
    state_hbm,
    gain_hbm,
    wq_hbm,
    wk_hbm,
    wv_hbm,
    wo_hbm,
    qgain_hbm,
    kgain_hbm,
    ck_hbm,
    cv_hbm,
    len_hbm,
    handed,
    nk_out,
    nv_out,
    state_v,
    gain_v,
    w_v,
    wo_v,
    qgain_v,
    kgain_v,
    ck_v,
    cv_v,
    len_v,
    partial_v,
    arrived_v,
    result_v,
    small_sem,
    w_sem,
    wo_sem,
    part_send,
    part_recv,
    res_send,
    res_recv,
):
    rows, width = state_v.shape
    heads = wq_hbm.shape[2] // HD
    depth = width // CHUNKS
    block = width // tensors
    slots = ck_v.shape[1]

    sec = lax.axis_index("section")
    ten = lax.axis_index("tensor")
    chip, core = ten // CORES, ten % CORES
    chips = tensors // CORES
    after = (sec + 1) % sections
    before = (sec + sections - 1) % sections

    offsets = [(dy, dc) for dy in range(1, chips) for dc in range(CORES)]
    offsets += [(0, dc) for dc in range(1, CORES)] + [(0, 0)]

    def member(offset):
        return ((chip + offset[0]) % chips) * CORES + (core + offset[1]) % CORES

    def origin(offset):
        return ((chip + chips - offset[0]) % chips) * CORES + (
            core + CORES - offset[1]
        ) % CORES

    def columns(which):
        return pl.ds(pl.multiple_of(which * block, 128), block)

    small = [
        pltpu.make_async_copy(source, target, small_sem.at[at])
        for at, (source, target) in enumerate(
            [
                (state_hbm.at[0], state_v),
                (gain_hbm, gain_v),
                (len_hbm, len_v),
                (qgain_hbm, qgain_v),
                (kgain_hbm, kgain_v),
                (ck_hbm.at[0, :, 0], ck_v),
                (cv_hbm.at[0, :, 0], cv_v),
            ]
        )
    ]
    for copy in small[:5]:
        copy.start()
    weights = []
    query_width = heads * HD
    for c in range(CHUNKS):
        span = pl.ds(c * depth, depth)
        weights.append(
            [
                pltpu.make_async_copy(
                    wq_hbm.at[0, span], w_v.at[span, pl.ds(0, query_width)], w_sem.at[c, 0]
                ),
                pltpu.make_async_copy(
                    wk_hbm.at[0, span], w_v.at[span, pl.ds(query_width, HD)], w_sem.at[c, 1]
                ),
                pltpu.make_async_copy(
                    wv_hbm.at[0, span], w_v.at[span, pl.ds(query_width + HD, HD)], w_sem.at[c, 2]
                ),
            ]
        )
        for copy in weights[-1]:
            copy.start()
    for copy in small[5:]:
        copy.start()
    projections = [
        pltpu.make_async_copy(
            wo_hbm.at[0, :, columns(member(offset))], wo_v.at[at], wo_sem.at[at]
        )
        for at, offset in enumerate(offsets)
    ]
    for copy in projections:
        copy.start()

    barrier = pltpu.get_barrier_semaphore()
    for offset in offsets[:-1]:
        pl.semaphore_signal(
            barrier, inc=1, device_id=(sec, member(offset)), device_id_type=MESH
        )
    for offset in offsets:
        pl.semaphore_signal(
            barrier, inc=1, device_id=(before, member(offset)), device_id_type=MESH
        )

    for copy in small[:5]:
        copy.wait()
    hidden = state_v[...].astype(jnp.float32)
    normed = (hidden * inverse_rms(hidden) * gain_v[...].astype(jnp.float32)).astype(jnp.bfloat16)

    on_diagonal = lax.broadcasted_iota(jnp.int32, (rows, rows), 0) == lax.broadcasted_iota(
        jnp.int32, (rows, rows), 1
    )
    spread = jnp.broadcast_to(len_v[...].astype(jnp.float32), (rows, rows))
    position = jnp.sum(jnp.where(on_diagonal, spread, 0.0), axis=1, keepdims=True)
    lane = lax.broadcasted_iota(jnp.int32, (rows, HD), 1)
    half = HD // 2
    index = jnp.where(lane < half, lane, lane - half).astype(jnp.float32)
    frequency = jnp.exp(index * (-2.0 / HD * 13.815510557964274))
    angles = position * frequency
    cosine = jnp.cos(angles)
    sine = jnp.sin(angles)
    sine = jnp.where(lane < half, -sine, sine)

    def rotate(values, cosines, sines):
        return values * cosines + pltpu.roll(values, half, 1) * sines

    gap = (
        lax.broadcasted_iota(jnp.int32, (rows, rows * slots), 1)
        - lax.broadcasted_iota(jnp.int32, (rows, rows * slots), 0) * slots
    ).astype(jnp.float32)
    excluded = jnp.where((gap >= 0.0) & (gap < position), 0.0, -1e30)

    def stacked(values):
        return jnp.concatenate([values] * heads, axis=0)

    cosine_all, sine_all, excluded_all = stacked(cosine), stacked(sine), stacked(excluded)
    query_gain = qgain_v[...].astype(jnp.float32)
    key_gain = kgain_v[...].astype(jnp.float32)

    total = None
    for c in range(CHUNKS):
        for copy in weights[c]:
            copy.wait()
        term = jnp.dot(
            normed[:, c * depth : (c + 1) * depth],
            w_v[c * depth : (c + 1) * depth, :],
            preferred_element_type=jnp.float32,
        )
        total = term if total is None else total + term

    key_raw = total[:, query_width : query_width + HD]
    new_value = total[:, query_width + HD :].astype(jnp.bfloat16)
    new_key = rotate(key_raw * inverse_rms(key_raw) * key_gain, cosine, sine).astype(jnp.bfloat16)
    nk_out[...] = new_key
    nv_out[...] = new_value

    query = jnp.concatenate([total[:, h * HD : (h + 1) * HD] for h in range(heads)], axis=0)
    query_rot = rotate(query * inverse_rms(query) * query_gain, cosine_all, sine_all).astype(
        jnp.bfloat16
    )

    scale = HD**-0.5
    own_score = (
        jnp.sum(
            query_rot.astype(jnp.float32) * stacked(new_key.astype(jnp.float32)),
            axis=1,
            keepdims=True,
        )
        * scale
    )
    small[5].wait()
    keys = ck_v[...].reshape(rows * slots, HD)
    scores = (
        lax.dot_general(
            query_rot, keys, (((1,), (1,)), ((), ())), preferred_element_type=jnp.float32
        )
        * scale
        + excluded_all
    )
    row_max = jnp.maximum(jnp.max(scores, axis=1, keepdims=True), own_score)
    cache_exp = jnp.exp(scores - row_max)
    own_exp = jnp.exp(own_score - row_max)
    share = 1.0 / (jnp.sum(cache_exp, axis=1, keepdims=True) + own_exp)
    cache_prob = (cache_exp * share).astype(jnp.bfloat16)
    own_prob = (own_exp * share).astype(jnp.bfloat16).astype(jnp.float32)
    small[6].wait()
    attended = jnp.dot(
        cache_prob, cv_v[...].reshape(rows * slots, HD), preferred_element_type=jnp.float32
    )
    attended = (attended + own_prob * stacked(new_value.astype(jnp.float32))).astype(jnp.bfloat16)
    attended = jnp.concatenate(
        [attended[h * rows : (h + 1) * rows] for h in range(heads)], axis=1
    )

    pl.semaphore_wait(barrier, 2 * tensors - 1)

    sends = []
    for at, offset in enumerate(offsets):
        projections[at].wait()
        partial = jnp.dot(attended, wo_v[at], preferred_element_type=jnp.float32)
        if at == tensors - 1:
            own = partial
            break
        partial_v[at] = partial
        send = pltpu.make_async_remote_copy(
            src_ref=partial_v.at[at],
            dst_ref=arrived_v.at[at],
            send_sem=part_send.at[at],
            recv_sem=part_recv.at[at],
            device_id=(sec, member(offset)),
            device_id_type=MESH,
        )
        send.start()
        sends.append(send)

    own = own + state_v[:, columns(ten)].astype(jnp.float32)
    for at in reversed(range(tensors - 1)):
        sends[at].wait_recv()
        own = own + arrived_v[at]
    result_v[...] = own.astype(jnp.bfloat16)

    def handing(at, offset, which):
        return pltpu.make_async_remote_copy(
            src_ref=result_v,
            dst_ref=handed.at[:, columns(which)],
            send_sem=res_send.at[at],
            recv_sem=res_recv.at[at],
            device_id=(after, member(offset)),
            device_id_type=MESH,
        )

    for at, offset in enumerate(offsets):
        handing(at, offset, ten).start()
    for send in sends:
        send.wait_send()
    for at, offset in enumerate(offsets):
        handing(at, offset, origin(offset)).wait_recv()
    for at, offset in enumerate(offsets):
        handing(at, offset, ten).wait_send()


def solution(mesh):
    sections, tensors = mesh.shape["section"], mesh.shape["tensor"]

    def body(state, gain_in, w_query, w_key, w_value, w_output, query_gain, key_gain, ck, cv, lengths):
        _, rows, width = state.shape
        query_width = w_query.shape[2]
        slots = ck.shape[3]
        block = width // tensors
        any_spec = pl.BlockSpec(memory_space=pltpu.HBM)
        vmem = pl.BlockSpec(memory_space=pltpu.VMEM)

        def kernel(*refs):
            tick_kernel(sections, tensors, *refs)

        handed, new_key, new_value = pl.pallas_call(
            kernel,
            out_shape=(
                jax.ShapeDtypeStruct((rows, width), jnp.bfloat16),
                jax.ShapeDtypeStruct((rows, HD), jnp.bfloat16),
                jax.ShapeDtypeStruct((rows, HD), jnp.bfloat16),
            ),
            in_specs=[any_spec] * 11,
            out_specs=(vmem, vmem, vmem),
            scratch_shapes=[
                pltpu.VMEM((rows, width), jnp.bfloat16),
                pltpu.VMEM((1, width), jnp.bfloat16),
                pltpu.VMEM((width, query_width + 2 * HD), jnp.bfloat16),
                pltpu.VMEM((tensors, query_width, block), jnp.bfloat16),
                pltpu.VMEM((1, HD), jnp.bfloat16),
                pltpu.VMEM((1, HD), jnp.bfloat16),
                pltpu.VMEM((rows, slots, HD), jnp.bfloat16),
                pltpu.VMEM((rows, slots, HD), jnp.bfloat16),
                pltpu.VMEM((1, rows), jnp.int32),
                pltpu.VMEM((tensors - 1, rows, block), jnp.float32),
                pltpu.VMEM((tensors - 1, rows, block), jnp.float32),
                pltpu.VMEM((rows, block), jnp.bfloat16),
                pltpu.SemaphoreType.DMA((7,)),
                pltpu.SemaphoreType.DMA((CHUNKS, 3)),
                pltpu.SemaphoreType.DMA((tensors,)),
                pltpu.SemaphoreType.DMA((tensors - 1,)),
                pltpu.SemaphoreType.DMA((tensors - 1,)),
                pltpu.SemaphoreType.DMA((tensors,)),
                pltpu.SemaphoreType.DMA((tensors,)),
            ],
            compiler_params=pltpu.CompilerParams(
                collective_id=0, has_side_effects=True, vmem_limit_bytes=63 * 1024 * 1024
            ),
            cost_estimate=pl.CostEstimate(
                flops=4 * rows * width * (query_width + HD),
                bytes_accessed=4 * width * (query_width + HD),
                transcendentals=rows * rows * slots * 8,
            ),
            name="tick",
        )(state, gain_in, w_query, w_key, w_value, w_output, query_gain, key_gain, ck, cv, lengths)
        return (
            handed[None],
            new_key.reshape(1, rows, 1, HD),
            new_value.reshape(1, rows, 1, HD),
        )

    placed = (
        P("section", None, None),
        P("section", None),
        P("section", None, "tensor"),
        P("section", None, "tensor"),
        P("section", None, "tensor"),
        P("section", "tensor", None),
        P("section", None),
        P("section", None),
        P("section", None, "tensor", None, None),
        P("section", None, "tensor", None, None),
        P("section", None),
    )
    return jax.shard_map(
        body,
        mesh=mesh,
        in_specs=placed,
        out_specs=(
            P("section", None, None),
            P("section", None, "tensor", None),
            P("section", None, "tensor", None),
        ),
        check_vma=False,
    )
```

```python
import jax
import jax.numpy as jnp
from jax import lax
from jax.experimental import pallas as pl
from jax.experimental.pallas import tpu as pltpu
from jax.sharding import PartitionSpec as P

HD = 128
CORES = 2
CHUNKS = 5
EPSILON = 1e-06
ROPE_BASE = 1000000.0
MESH = pl.DeviceIdType.MESH


def inverse_rms(values):
    return lax.rsqrt(jnp.mean(values * values, axis=-1, keepdims=True) + EPSILON)


def tick_kernel(
    sections,
    tensors,
    state_hbm,
    gain_hbm,
    wq_hbm,
    wk_hbm,
    wv_hbm,
    wo_hbm,
    qgain_hbm,
    kgain_hbm,
    ck_hbm,
    cv_hbm,
    len_hbm,
    handed,
    nk_out,
    nv_out,
    state_v,
    gain_v,
    w_v,
    wo_v,
    qgain_v,
    kgain_v,
    ck_v,
    cv_v,
    len_v,
    partial_v,
    arrived_v,
    result_v,
    small_sem,
    w_sem,
    wo_sem,
    part_send,
    part_recv,
    res_send,
    res_recv,
):
    rows, width = state_v.shape
    heads = wq_hbm.shape[2] // HD
    depth = width // CHUNKS
    block = width // tensors
    slots = ck_v.shape[1]

    sec = lax.axis_index("section")
    ten = lax.axis_index("tensor")
    chip, core = ten // CORES, ten % CORES
    chips = tensors // CORES
    after = (sec + 1) % sections
    before = (sec + sections - 1) % sections

    offsets = [(dy, dc) for dy in range(1, chips) for dc in range(CORES)]
    offsets += [(0, dc) for dc in range(1, CORES)] + [(0, 0)]

    def member(offset):
        return ((chip + offset[0]) % chips) * CORES + (core + offset[1]) % CORES

    def origin(offset):
        return ((chip + chips - offset[0]) % chips) * CORES + (
            core + CORES - offset[1]
        ) % CORES

    def columns(which):
        return pl.ds(pl.multiple_of(which * block, 128), block)

    small = [
        pltpu.make_async_copy(source, target, small_sem.at[at])
        for at, (source, target) in enumerate(
            [
                (state_hbm.at[0], state_v),
                (gain_hbm, gain_v),
                (len_hbm, len_v),
                (qgain_hbm, qgain_v),
                (kgain_hbm, kgain_v),
                (ck_hbm.at[0, :, 0], ck_v),
                (cv_hbm.at[0, :, 0], cv_v),
            ]
        )
    ]
    for copy in small[:5]:
        copy.start()
    weights = []
    query_width = heads * HD
    for c in range(CHUNKS):
        span = pl.ds(c * depth, depth)
        weights.append(
            [
                pltpu.make_async_copy(
                    wq_hbm.at[0, span], w_v.at[span, pl.ds(0, query_width)], w_sem.at[c, 0]
                ),
                pltpu.make_async_copy(
                    wk_hbm.at[0, span], w_v.at[span, pl.ds(query_width, HD)], w_sem.at[c, 1]
                ),
                pltpu.make_async_copy(
                    wv_hbm.at[0, span], w_v.at[span, pl.ds(query_width + HD, HD)], w_sem.at[c, 2]
                ),
            ]
        )
        for copy in weights[-1]:
            copy.start()
    for copy in small[5:]:
        copy.start()
    projections = [
        pltpu.make_async_copy(
            wo_hbm.at[0, :, columns(member(offset))], wo_v.at[at], wo_sem.at[at]
        )
        for at, offset in enumerate(offsets)
    ]
    for copy in projections:
        copy.start()

    barrier = pltpu.get_barrier_semaphore()
    for offset in offsets[:-1]:
        pl.semaphore_signal(
            barrier, inc=1, device_id=(sec, member(offset)), device_id_type=MESH
        )
    for offset in offsets:
        pl.semaphore_signal(
            barrier, inc=1, device_id=(before, member(offset)), device_id_type=MESH
        )

    for copy in small[:5]:
        copy.wait()
    hidden = state_v[...].astype(jnp.float32)
    normed = (hidden * inverse_rms(hidden) * gain_v[...].astype(jnp.float32)).astype(jnp.bfloat16)

    on_diagonal = lax.broadcasted_iota(jnp.int32, (rows, rows), 0) == lax.broadcasted_iota(
        jnp.int32, (rows, rows), 1
    )
    spread = jnp.broadcast_to(len_v[...].astype(jnp.float32), (rows, rows))
    position = jnp.sum(jnp.where(on_diagonal, spread, 0.0), axis=1, keepdims=True)
    lane = lax.broadcasted_iota(jnp.int32, (rows, HD), 1)
    half = HD // 2
    index = jnp.where(lane < half, lane, lane - half).astype(jnp.float32)
    frequency = jnp.exp(index * (-2.0 / HD * 13.815510557964274))
    angles = position * frequency
    cosine = jnp.cos(angles)
    sine = jnp.sin(angles)
    sine = jnp.where(lane < half, -sine, sine)

    def rotate(values, cosines, sines):
        return values * cosines + pltpu.roll(values, half, 1) * sines

    gap = (
        lax.broadcasted_iota(jnp.int32, (rows, rows * slots), 1)
        - lax.broadcasted_iota(jnp.int32, (rows, rows * slots), 0) * slots
    ).astype(jnp.float32)
    excluded = jnp.where((gap >= 0.0) & (gap < position), 0.0, -1e30)

    def stacked(values):
        return jnp.concatenate([values] * heads, axis=0)

    cosine_all, sine_all, excluded_all = stacked(cosine), stacked(sine), stacked(excluded)
    query_gain = qgain_v[...].astype(jnp.float32)
    key_gain = kgain_v[...].astype(jnp.float32)

    total = None
    for c in range(CHUNKS):
        for copy in weights[c]:
            copy.wait()
        term = jnp.dot(
            normed[:, c * depth : (c + 1) * depth],
            w_v[c * depth : (c + 1) * depth, :],
            preferred_element_type=jnp.float32,
        )
        total = term if total is None else total + term

    key_raw = total[:, query_width : query_width + HD]
    new_value = total[:, query_width + HD :].astype(jnp.bfloat16)
    new_key = rotate(key_raw * inverse_rms(key_raw) * key_gain, cosine, sine).astype(jnp.bfloat16)
    nk_out[...] = new_key
    nv_out[...] = new_value

    query = jnp.concatenate([total[:, h * HD : (h + 1) * HD] for h in range(heads)], axis=0)
    query_rot = rotate(query * inverse_rms(query) * query_gain, cosine_all, sine_all).astype(
        jnp.bfloat16
    )

    scale = HD**-0.5
    own_score = (
        jnp.sum(
            query_rot.astype(jnp.float32) * stacked(new_key.astype(jnp.float32)),
            axis=1,
            keepdims=True,
        )
        * scale
    )
    small[5].wait()
    keys = ck_v[...].reshape(rows * slots, HD)
    scores = (
        lax.dot_general(
            query_rot, keys, (((1,), (1,)), ((), ())), preferred_element_type=jnp.float32
        )
        * scale
        + excluded_all
    )
    row_max = jnp.maximum(jnp.max(scores, axis=1, keepdims=True), own_score)
    cache_exp = jnp.exp(scores - row_max)
    own_exp = jnp.exp(own_score - row_max)
    share = 1.0 / (jnp.sum(cache_exp, axis=1, keepdims=True) + own_exp)
    cache_prob = (cache_exp * share).astype(jnp.bfloat16)
    own_prob = (own_exp * share).astype(jnp.bfloat16).astype(jnp.float32)
    small[6].wait()
    attended = jnp.dot(
        cache_prob, cv_v[...].reshape(rows * slots, HD), preferred_element_type=jnp.float32
    )
    attended = (attended + own_prob * stacked(new_value.astype(jnp.float32))).astype(jnp.bfloat16)
    attended = jnp.concatenate(
        [attended[h * rows : (h + 1) * rows] for h in range(heads)], axis=1
    )

    pl.semaphore_wait(barrier, 2 * tensors - 1)

    sends = []
    for at, offset in enumerate(offsets):
        projections[at].wait()
        partial = jnp.dot(attended, wo_v[at], preferred_element_type=jnp.float32)
        if at == tensors - 1:
            own = partial
            break
        partial_v[at] = partial
        send = pltpu.make_async_remote_copy(
            src_ref=partial_v.at[at],
            dst_ref=arrived_v.at[at],
            send_sem=part_send.at[at],
            recv_sem=part_recv.at[at],
            device_id=(sec, member(offset)),
            device_id_type=MESH,
        )
        send.start()
        sends.append(send)

    own = own + state_v[:, columns(ten)].astype(jnp.float32)
    for at in reversed(range(tensors - 1)):
        sends[at].wait_recv()
        own = own + arrived_v[at]
    result_v[...] = own.astype(jnp.bfloat16)

    def handing(at, offset, which):
        return pltpu.make_async_remote_copy(
            src_ref=result_v,
            dst_ref=handed.at[:, columns(which)],
            send_sem=res_send.at[at],
            recv_sem=res_recv.at[at],
            device_id=(after, member(offset)),
            device_id_type=MESH,
        )

    for at, offset in enumerate(offsets):
        handing(at, offset, ten).start()
    for send in sends:
        send.wait_send()
    for at, offset in enumerate(offsets):
        handing(at, offset, origin(offset)).wait_recv()
    for at, offset in enumerate(offsets):
        handing(at, offset, ten).wait_send()


def store_kernel(*refs):
    count = (len(refs) - 1) // 2
    copies = [
        pltpu.make_async_copy(refs[at], refs[count + at], refs[-1].at[at]) for at in range(count)
    ]
    for copy in copies:
        copy.start()
    for copy in copies:
        copy.wait()


def solution(mesh):
    sections, tensors = mesh.shape["section"], mesh.shape["tensor"]

    def body(state, gain_in, w_query, w_key, w_value, w_output, query_gain, key_gain, ck, cv, lengths):
        _, rows, width = state.shape
        query_width = w_query.shape[2]
        slots = ck.shape[3]
        block = width // tensors
        hbm = pl.BlockSpec(memory_space=pltpu.HBM)
        vmem = pl.BlockSpec(memory_space=pltpu.VMEM)

        def kernel(*refs):
            tick_kernel(sections, tensors, *refs)

        operands = (
            state, gain_in, w_query, w_key, w_value, w_output, query_gain, key_gain, ck, cv, lengths
        )
        operands = [pltpu.with_memory_space_constraint(x, pltpu.HBM) for x in operands]
        shapes = ((rows, width), (rows, HD), (rows, HD))
        results = pl.pallas_call(
            kernel,
            out_shape=tuple(pltpu.VMEM(shape, jnp.bfloat16) for shape in shapes),
            in_specs=[hbm] * 11,
            out_specs=(vmem, vmem, vmem),
            scratch_shapes=[
                pltpu.VMEM((rows, width), jnp.bfloat16),
                pltpu.VMEM((1, width), jnp.bfloat16),
                pltpu.VMEM((width, query_width + 2 * HD), jnp.bfloat16),
                pltpu.VMEM((tensors, query_width, block), jnp.bfloat16),
                pltpu.VMEM((1, HD), jnp.bfloat16),
                pltpu.VMEM((1, HD), jnp.bfloat16),
                pltpu.VMEM((rows, slots, HD), jnp.bfloat16),
                pltpu.VMEM((rows, slots, HD), jnp.bfloat16),
                pltpu.VMEM((1, rows), jnp.int32),
                pltpu.VMEM((tensors - 1, rows, block), jnp.float32),
                pltpu.VMEM((tensors - 1, rows, block), jnp.float32),
                pltpu.VMEM((rows, block), jnp.bfloat16),
                pltpu.SemaphoreType.DMA((7,)),
                pltpu.SemaphoreType.DMA((CHUNKS, 3)),
                pltpu.SemaphoreType.DMA((tensors,)),
                pltpu.SemaphoreType.DMA((tensors - 1,)),
                pltpu.SemaphoreType.DMA((tensors - 1,)),
                pltpu.SemaphoreType.DMA((tensors,)),
                pltpu.SemaphoreType.DMA((tensors,)),
            ],
            compiler_params=pltpu.CompilerParams(
                collective_id=0, has_side_effects=True, vmem_limit_bytes=48 * 1024 * 1024
            ),
            cost_estimate=pl.CostEstimate(
                flops=4 * rows * width * (query_width + HD),
                bytes_accessed=4 * width * (query_width + HD),
                transcendentals=rows * rows * slots * 8,
            ),
            name="tick",
        )(*operands)
        handed, new_key, new_value = pl.pallas_call(
            store_kernel,
            out_shape=tuple(pltpu.HBM(shape, jnp.bfloat16) for shape in shapes),
            in_specs=[vmem] * 3,
            out_specs=(hbm, hbm, hbm),
            scratch_shapes=[pltpu.SemaphoreType.DMA((3,))],
            compiler_params=pltpu.CompilerParams(vmem_limit_bytes=8 * 1024 * 1024),
            name="store",
        )(*results)
        return (
            handed[None],
            new_key.reshape(1, rows, 1, HD),
            new_value.reshape(1, rows, 1, HD),
        )

    placed = (
        P("section", None, None),
        P("section", None),
        P("section", None, "tensor"),
        P("section", None, "tensor"),
        P("section", None, "tensor"),
        P("section", "tensor", None),
        P("section", None),
        P("section", None),
        P("section", None, "tensor", None, None),
        P("section", None, "tensor", None, None),
        P("section", None),
    )
    return jax.shard_map(
        body,
        mesh=mesh,
        in_specs=placed,
        out_specs=(
            P("section", None, None),
            P("section", None, "tensor", None),
            P("section", None, "tensor", None),
        ),
        check_vma=False,
    )
```

```python
import jax
import jax.numpy as jnp
from jax import lax
from jax.experimental import pallas as pl
from jax.experimental.pallas import tpu as pltpu
from jax.sharding import PartitionSpec as P

HD = 128
CORES = 2
CHUNKS = 5
EPSILON = 1e-06
ROPE_BASE = 1000000.0
MESH = pl.DeviceIdType.MESH


def inverse_rms(values):
    return lax.rsqrt(jnp.mean(values * values, axis=-1, keepdims=True) + EPSILON)


def part_starts(block):
    first = block // 128 * 2 // 5 * 128
    return ((0, first), (first, block - first))


def tick_kernel(
    sections,
    tensors,
    state_hbm,
    gain_hbm,
    wq_hbm,
    wk_hbm,
    wv_hbm,
    wo_hbm,
    qgain_hbm,
    kgain_hbm,
    ck_hbm,
    cv_hbm,
    len_hbm,
    handed,
    nk_out,
    nv_out,
    state_v,
    gain_v,
    w_v,
    wo_v,
    qgain_v,
    kgain_v,
    ck_v,
    cv_v,
    len_v,
    far_v,
    far_arrived_v,
    near_v,
    near_arrived_v,
    result_v,
    small_sem,
    w_sem,
    wo_sem,
    part_send,
    part_recv,
    res_send,
    res_recv,
):
    rows, width = state_v.shape
    heads = wq_hbm.shape[2] // HD
    depth = width // CHUNKS
    block = width // tensors
    slots = ck_v.shape[1]

    sec = lax.axis_index("section")
    ten = lax.axis_index("tensor")
    chip, core = ten // CORES, ten % CORES
    chips = tensors // CORES
    after = (sec + 1) % sections
    before = (sec + sections - 1) % sections

    offsets = [(dy, dc) for dy in range(1, chips) for dc in range(CORES)]
    offsets += [(0, dc) for dc in range(1, CORES)] + [(0, 0)]

    def member(offset):
        return ((chip + offset[0]) % chips) * CORES + (core + offset[1]) % CORES

    def origin(offset):
        return ((chip + chips - offset[0]) % chips) * CORES + (
            core + CORES - offset[1]
        ) % CORES

    def columns(which):
        return pl.ds(pl.multiple_of(which * block, 128), block)

    small = [
        pltpu.make_async_copy(source, target, small_sem.at[at])
        for at, (source, target) in enumerate(
            [
                (state_hbm.at[0], state_v),
                (gain_hbm, gain_v),
                (len_hbm, len_v),
                (qgain_hbm, qgain_v),
                (kgain_hbm, kgain_v),
                (ck_hbm.at[0, :, 0], ck_v),
                (cv_hbm.at[0, :, 0], cv_v),
            ]
        )
    ]
    for copy in small[:5]:
        copy.start()
    weights = []
    query_width = heads * HD
    for c in range(CHUNKS):
        span = pl.ds(c * depth, depth)
        weights.append(
            [
                pltpu.make_async_copy(
                    wq_hbm.at[0, span], w_v.at[span, pl.ds(0, query_width)], w_sem.at[c, 0]
                ),
                pltpu.make_async_copy(
                    wk_hbm.at[0, span], w_v.at[span, pl.ds(query_width, HD)], w_sem.at[c, 1]
                ),
                pltpu.make_async_copy(
                    wv_hbm.at[0, span], w_v.at[span, pl.ds(query_width + HD, HD)], w_sem.at[c, 2]
                ),
            ]
        )
        for copy in weights[-1]:
            copy.start()
    for copy in small[5:]:
        copy.start()
    projections = [
        pltpu.make_async_copy(
            wo_hbm.at[0, :, columns(member(offset))], wo_v.at[at], wo_sem.at[at]
        )
        for at, offset in enumerate(offsets)
    ]
    for copy in projections:
        copy.start()

    barrier = pltpu.get_barrier_semaphore()
    for offset in offsets[:-1]:
        pl.semaphore_signal(
            barrier, inc=1, device_id=(sec, member(offset)), device_id_type=MESH
        )
    for offset in offsets:
        pl.semaphore_signal(
            barrier, inc=1, device_id=(before, member(offset)), device_id_type=MESH
        )

    for copy in small[:5]:
        copy.wait()
    hidden = state_v[...].astype(jnp.float32)
    normed = (hidden * inverse_rms(hidden) * gain_v[...].astype(jnp.float32)).astype(jnp.bfloat16)

    on_diagonal = lax.broadcasted_iota(jnp.int32, (rows, rows), 0) == lax.broadcasted_iota(
        jnp.int32, (rows, rows), 1
    )
    spread = jnp.broadcast_to(len_v[...].astype(jnp.float32), (rows, rows))
    position = jnp.sum(jnp.where(on_diagonal, spread, 0.0), axis=1, keepdims=True)
    lane = lax.broadcasted_iota(jnp.int32, (rows, HD), 1)
    half = HD // 2
    index = jnp.where(lane < half, lane, lane - half).astype(jnp.float32)
    frequency = jnp.exp(index * (-2.0 / HD * 13.815510557964274))
    angles = position * frequency
    cosine = jnp.cos(angles)
    sine = jnp.sin(angles)
    sine = jnp.where(lane < half, -sine, sine)

    def rotate(values, cosines, sines):
        return values * cosines + pltpu.roll(values, half, 1) * sines

    gap = (
        lax.broadcasted_iota(jnp.int32, (rows, rows * slots), 1)
        - lax.broadcasted_iota(jnp.int32, (rows, rows * slots), 0) * slots
    ).astype(jnp.float32)
    excluded = jnp.where((gap >= 0.0) & (gap < position), 0.0, -1e30)

    def stacked(values):
        return jnp.concatenate([values] * heads, axis=0)

    cosine_all, sine_all, excluded_all = stacked(cosine), stacked(sine), stacked(excluded)
    query_gain = qgain_v[...].astype(jnp.float32)
    key_gain = kgain_v[...].astype(jnp.float32)

    total = None
    for c in range(CHUNKS):
        for copy in weights[c]:
            copy.wait()
        term = jnp.dot(
            normed[:, c * depth : (c + 1) * depth],
            w_v[c * depth : (c + 1) * depth, :],
            preferred_element_type=jnp.float32,
        )
        total = term if total is None else total + term

    key_raw = total[:, query_width : query_width + HD]
    new_value = total[:, query_width + HD :].astype(jnp.bfloat16)
    new_key = rotate(key_raw * inverse_rms(key_raw) * key_gain, cosine, sine).astype(jnp.bfloat16)
    nk_out[...] = new_key
    nv_out[...] = new_value

    query = jnp.concatenate([total[:, h * HD : (h + 1) * HD] for h in range(heads)], axis=0)
    query_rot = rotate(query * inverse_rms(query) * query_gain, cosine_all, sine_all).astype(
        jnp.bfloat16
    )

    scale = HD**-0.5
    own_score = (
        jnp.sum(
            query_rot.astype(jnp.float32) * stacked(new_key.astype(jnp.float32)),
            axis=1,
            keepdims=True,
        )
        * scale
    )
    small[5].wait()
    keys = ck_v[...].reshape(rows * slots, HD)
    scores = (
        lax.dot_general(
            query_rot, keys, (((1,), (1,)), ((), ())), preferred_element_type=jnp.float32
        )
        * scale
        + excluded_all
    )
    row_max = jnp.maximum(jnp.max(scores, axis=1, keepdims=True), own_score)
    cache_exp = jnp.exp(scores - row_max)
    own_exp = jnp.exp(own_score - row_max)
    share = 1.0 / (jnp.sum(cache_exp, axis=1, keepdims=True) + own_exp)
    cache_prob = (cache_exp * share).astype(jnp.bfloat16)
    own_prob = (own_exp * share).astype(jnp.bfloat16).astype(jnp.float32)
    small[6].wait()
    attended = jnp.dot(
        cache_prob, cv_v[...].reshape(rows * slots, HD), preferred_element_type=jnp.float32
    )
    attended = (attended + own_prob * stacked(new_value.astype(jnp.float32))).astype(jnp.bfloat16)
    attended = jnp.concatenate(
        [attended[h * rows : (h + 1) * rows] for h in range(heads)], axis=1
    )

    pl.semaphore_wait(barrier, 2 * tensors - 1)

    far = tensors - CORES
    starts = part_starts(block)
    sends, own = [], []
    for part, (start, size) in enumerate(starts):
        sends.append([])
        for at, offset in enumerate(offsets):
            if part == 0:
                projections[at].wait()
            partial = jnp.dot(
                attended, wo_v[at, :, start : start + size], preferred_element_type=jnp.float32
            )
            if at == tensors - 1:
                own.append(partial)
                break
            if at < far:
                source, target = far_v[part].at[at], far_arrived_v[part].at[at]
            else:
                source, target = near_v[part].at[at - far], near_arrived_v[part].at[at - far]
            source[...] = partial.astype(source.dtype)
            send = pltpu.make_async_remote_copy(
                src_ref=source,
                dst_ref=target,
                send_sem=part_send.at[part, at],
                recv_sem=part_recv.at[part, at],
                device_id=(sec, member(offset)),
                device_id_type=MESH,
            )
            send.start()
            sends[-1].append((send, target))

    def handing(part, at, offset, which):
        start, size = starts[part]
        span = pl.ds(pl.multiple_of(which * block + start, 128), size)
        return pltpu.make_async_remote_copy(
            src_ref=result_v[part],
            dst_ref=handed.at[:, span],
            send_sem=res_send.at[part, at],
            recv_sem=res_recv.at[part, at],
            device_id=(after, member(offset)),
            device_id_type=MESH,
        )

    for part, (start, size) in enumerate(starts):
        span = pl.ds(pl.multiple_of(ten * block + start, 128), size)
        result = own[part] + state_v[:, span].astype(jnp.float32)
        for send, target in reversed(sends[part]):
            send.wait_recv()
            result = result + target[...].astype(jnp.float32)
        result_v[part][...] = result.astype(jnp.bfloat16)
        for at, offset in enumerate(offsets):
            handing(part, at, offset, ten).start()
    for part in range(len(starts)):
        for send, _ in sends[part]:
            send.wait_send()
    for part in range(len(starts)):
        for at, offset in enumerate(offsets):
            handing(part, at, offset, origin(offset)).wait_recv()
    for part in range(len(starts)):
        for at, offset in enumerate(offsets):
            handing(part, at, offset, ten).wait_send()


def store_kernel(*refs):
    count = (len(refs) - 1) // 2
    copies = [
        pltpu.make_async_copy(refs[at], refs[count + at], refs[-1].at[at]) for at in range(count)
    ]
    for copy in copies:
        copy.start()
    for copy in copies:
        copy.wait()


def solution(mesh):
    sections, tensors = mesh.shape["section"], mesh.shape["tensor"]

    def body(state, gain_in, w_query, w_key, w_value, w_output, query_gain, key_gain, ck, cv, lengths):
        _, rows, width = state.shape
        query_width = w_query.shape[2]
        slots = ck.shape[3]
        block = width // tensors
        far = tensors - CORES
        sizes = [size for _, size in part_starts(block)]
        hbm = pl.BlockSpec(memory_space=pltpu.HBM)
        vmem = pl.BlockSpec(memory_space=pltpu.VMEM)

        def kernel(*refs):
            tick_kernel(sections, tensors, *refs)

        operands = (
            state, gain_in, w_query, w_key, w_value, w_output, query_gain, key_gain, ck, cv, lengths
        )
        operands = [pltpu.with_memory_space_constraint(x, pltpu.HBM) for x in operands]
        shapes = ((rows, width), (rows, HD), (rows, HD))
        results = pl.pallas_call(
            kernel,
            out_shape=tuple(pltpu.VMEM(shape, jnp.bfloat16) for shape in shapes),
            in_specs=[hbm] * 11,
            out_specs=(vmem, vmem, vmem),
            scratch_shapes=[
                pltpu.VMEM((rows, width), jnp.bfloat16),
                pltpu.VMEM((1, width), jnp.bfloat16),
                pltpu.VMEM((width, query_width + 2 * HD), jnp.bfloat16),
                pltpu.VMEM((tensors, query_width, block), jnp.bfloat16),
                pltpu.VMEM((1, HD), jnp.bfloat16),
                pltpu.VMEM((1, HD), jnp.bfloat16),
                pltpu.VMEM((rows, slots, HD), jnp.bfloat16),
                pltpu.VMEM((rows, slots, HD), jnp.bfloat16),
                pltpu.VMEM((1, rows), jnp.int32),
                [pltpu.VMEM((far, rows, size), jnp.bfloat16) for size in sizes],
                [pltpu.VMEM((far, rows, size), jnp.bfloat16) for size in sizes],
                [pltpu.VMEM((CORES - 1, rows, size), jnp.float32) for size in sizes],
                [pltpu.VMEM((CORES - 1, rows, size), jnp.float32) for size in sizes],
                [pltpu.VMEM((rows, size), jnp.bfloat16) for size in sizes],
                pltpu.SemaphoreType.DMA((7,)),
                pltpu.SemaphoreType.DMA((CHUNKS, 3)),
                pltpu.SemaphoreType.DMA((tensors,)),
                pltpu.SemaphoreType.DMA((len(sizes), tensors - 1)),
                pltpu.SemaphoreType.DMA((len(sizes), tensors - 1)),
                pltpu.SemaphoreType.DMA((len(sizes), tensors)),
                pltpu.SemaphoreType.DMA((len(sizes), tensors)),
            ],
            compiler_params=pltpu.CompilerParams(
                collective_id=0, has_side_effects=True, vmem_limit_bytes=48 * 1024 * 1024
            ),
            cost_estimate=pl.CostEstimate(
                flops=4 * rows * width * (query_width + HD),
                bytes_accessed=4 * width * (query_width + HD),
                transcendentals=rows * rows * slots * 8,
            ),
            name="tick",
        )(*operands)
        handed, new_key, new_value = pl.pallas_call(
            store_kernel,
            out_shape=tuple(pltpu.HBM(shape, jnp.bfloat16) for shape in shapes),
            in_specs=[vmem] * 3,
            out_specs=(hbm, hbm, hbm),
            scratch_shapes=[pltpu.SemaphoreType.DMA((3,))],
            compiler_params=pltpu.CompilerParams(vmem_limit_bytes=8 * 1024 * 1024),
            name="store",
        )(*results)
        return (
            handed[None],
            new_key.reshape(1, rows, 1, HD),
            new_value.reshape(1, rows, 1, HD),
        )

    placed = (
        P("section", None, None),
        P("section", None),
        P("section", None, "tensor"),
        P("section", None, "tensor"),
        P("section", None, "tensor"),
        P("section", "tensor", None),
        P("section", None),
        P("section", None),
        P("section", None, "tensor", None, None),
        P("section", None, "tensor", None, None),
        P("section", None),
    )
    return jax.shard_map(
        body,
        mesh=mesh,
        in_specs=placed,
        out_specs=(
            P("section", None, None),
            P("section", None, "tensor", None),
            P("section", None, "tensor", None),
        ),
        check_vma=False,
    )
```

```python
import jax
import jax.numpy as jnp
from jax import lax
from jax.experimental import pallas as pl
from jax.experimental.pallas import tpu as pltpu
from jax.sharding import PartitionSpec as P

HD = 128
CORES = 2
GROUPS = 2
EPSILON = 1e-06
ROPE_BASE = 1000000.0
MESH = pl.DeviceIdType.MESH


def inverse_rms(values):
    return lax.rsqrt(jnp.mean(values * values, axis=-1, keepdims=True) + EPSILON)


def tick_kernel(
    sections,
    tensors,
    state_hbm,
    gain_hbm,
    wq_hbm,
    wk_hbm,
    wv_hbm,
    wo_hbm,
    qgain_hbm,
    kgain_hbm,
    ck_hbm,
    cv_hbm,
    len_hbm,
    handed,
    nk_out,
    nv_out,
    state_v,
    gain_v,
    wkv_v,
    wq_v,
    wo_v,
    qgain_v,
    kgain_v,
    ck_v,
    cv_v,
    len_v,
    total_v,
    arrived_v,
    result_v,
    small_sem,
    wkv_sem,
    wq_sem,
    wo_sem,
    part_send,
    part_recv,
    res_send,
    res_recv,
):
    rows, width = state_v.shape
    heads = wq_hbm.shape[2] // HD
    members = heads // GROUPS
    span = members * HD
    block = width // tensors
    slots = ck_v.shape[1]

    sec = lax.axis_index("section")
    ten = lax.axis_index("tensor")
    chip, core = ten // CORES, ten % CORES
    chips = tensors // CORES
    after = (sec + 1) % sections
    before = (sec + sections - 1) % sections

    offsets = [(dy, dc) for dy in range(1, chips) for dc in range(CORES)]
    offsets += [(0, dc) for dc in range(1, CORES)] + [(0, 0)]

    def member(offset):
        return ((chip + offset[0]) % chips) * CORES + (core + offset[1]) % CORES

    def origin(offset):
        return ((chip + chips - offset[0]) % chips) * CORES + (
            core + CORES - offset[1]
        ) % CORES

    def columns(which):
        return pl.ds(pl.multiple_of(which * block, 128), block)

    small = [
        pltpu.make_async_copy(source, target, small_sem.at[at])
        for at, (source, target) in enumerate(
            [
                (state_hbm.at[0], state_v),
                (gain_hbm, gain_v),
                (len_hbm, len_v),
                (qgain_hbm, qgain_v),
                (kgain_hbm, kgain_v),
                (ck_hbm.at[0, :, 0], ck_v),
                (cv_hbm.at[0, :, 0], cv_v),
            ]
        )
    ]
    for copy in small[:5]:
        copy.start()
    pair = [
        pltpu.make_async_copy(source.at[0], wkv_v.at[:, pl.ds(at * HD, HD)], wkv_sem.at[at])
        for at, source in enumerate((wk_hbm, wv_hbm))
    ]
    queries = [
        pltpu.make_async_copy(wq_hbm.at[0, :, pl.ds(g * span, span)], wq_v.at[g], wq_sem.at[g])
        for g in range(GROUPS)
    ]
    projections = [
        pltpu.make_async_copy(wo_hbm.at[0, pl.ds(g * span, span)], wo_v.at[g], wo_sem.at[g])
        for g in range(GROUPS)
    ]
    for copy in pair + queries[:1] + small[5:]:
        copy.start()
    for g in range(GROUPS):
        if g + 1 < GROUPS:
            queries[g + 1].start()
        projections[g].start()

    barrier = pltpu.get_barrier_semaphore()
    for offset in offsets[:-1]:
        pl.semaphore_signal(
            barrier, inc=1, device_id=(sec, member(offset)), device_id_type=MESH
        )
    for offset in offsets:
        pl.semaphore_signal(
            barrier, inc=1, device_id=(before, member(offset)), device_id_type=MESH
        )

    for copy in small[:5]:
        copy.wait()
    hidden = state_v[...].astype(jnp.float32)
    normed = (hidden * inverse_rms(hidden) * gain_v[...].astype(jnp.float32)).astype(jnp.bfloat16)

    on_diagonal = lax.broadcasted_iota(jnp.int32, (rows, rows), 0) == lax.broadcasted_iota(
        jnp.int32, (rows, rows), 1
    )
    spread = jnp.broadcast_to(len_v[...].astype(jnp.float32), (rows, rows))
    position = jnp.sum(jnp.where(on_diagonal, spread, 0.0), axis=1, keepdims=True)
    lane = lax.broadcasted_iota(jnp.int32, (rows, HD), 1)
    half = HD // 2
    index = jnp.where(lane < half, lane, lane - half).astype(jnp.float32)
    frequency = jnp.exp(index * (-2.0 / HD * 13.815510557964274))
    angles = position * frequency
    cosine = jnp.cos(angles)
    sine = jnp.sin(angles)
    sine = jnp.where(lane < half, -sine, sine)

    def rotate(values, cosines, sines):
        return values * cosines + pltpu.roll(values, half, 1) * sines

    gap = (
        lax.broadcasted_iota(jnp.int32, (rows, rows * slots), 1)
        - lax.broadcasted_iota(jnp.int32, (rows, rows * slots), 0) * slots
    ).astype(jnp.float32)
    excluded = jnp.where((gap >= 0.0) & (gap < position), 0.0, -1e30)

    def stacked(values):
        return jnp.concatenate([values] * members, axis=0)

    cosine_all, sine_all, excluded_all = stacked(cosine), stacked(sine), stacked(excluded)
    query_gain = qgain_v[...].astype(jnp.float32)
    key_gain = kgain_v[...].astype(jnp.float32)

    def project(g):
        queries[g].wait()
        return jnp.dot(normed, wq_v[g], preferred_element_type=jnp.float32)

    for copy in pair:
        copy.wait()
    both = jnp.dot(normed, wkv_v[...], preferred_element_type=jnp.float32)
    query = project(0)
    key_raw = both[:, :HD]
    new_value = both[:, HD:].astype(jnp.bfloat16)
    new_key = rotate(key_raw * inverse_rms(key_raw) * key_gain, cosine, sine).astype(jnp.bfloat16)
    nk_out[...] = new_key
    nv_out[...] = new_value
    own_keys = stacked(new_key.astype(jnp.float32))
    own_values = stacked(new_value.astype(jnp.float32))
    for copy in small[5:]:
        copy.wait()

    scale = HD**-0.5

    def attend(query):
        query = jnp.concatenate([query[:, h * HD : (h + 1) * HD] for h in range(members)], axis=0)
        query_rot = rotate(query * inverse_rms(query) * query_gain, cosine_all, sine_all).astype(
            jnp.bfloat16
        )
        own_score = (
            jnp.sum(query_rot.astype(jnp.float32) * own_keys, axis=1, keepdims=True) * scale
        )
        scores = (
            lax.dot_general(
                query_rot,
                ck_v[...].reshape(rows * slots, HD),
                (((1,), (1,)), ((), ())),
                preferred_element_type=jnp.float32,
            )
            * scale
            + excluded_all
        )
        row_max = jnp.maximum(jnp.max(scores, axis=1, keepdims=True), own_score)
        cache_exp = jnp.exp(scores - row_max)
        own_exp = jnp.exp(own_score - row_max)
        share = 1.0 / (jnp.sum(cache_exp, axis=1, keepdims=True) + own_exp)
        cache_prob = (cache_exp * share).astype(jnp.bfloat16)
        own_prob = (own_exp * share).astype(jnp.bfloat16).astype(jnp.float32)
        attended = jnp.dot(
            cache_prob, cv_v[...].reshape(rows * slots, HD), preferred_element_type=jnp.float32
        )
        attended = (attended + own_prob * own_values).astype(jnp.bfloat16)
        return jnp.concatenate(
            [attended[h * rows : (h + 1) * rows] for h in range(members)], axis=1
        )

    attended = None
    for g in range(GROUPS + 1):
        if 0 < g:
            projections[g - 1].wait()
        later = project(g + 1) if g + 1 < GROUPS else None
        if 0 < g:
            term = jnp.dot(attended, wo_v[g - 1], preferred_element_type=jnp.float32)
            total_v[...] = term if g == 1 else total_v[...] + term
        if g < GROUPS:
            attended = attend(query)
        query = later

    pl.semaphore_wait(barrier, 2 * tensors - 1)

    sends = []
    for at, offset in enumerate(offsets[:-1]):
        send = pltpu.make_async_remote_copy(
            src_ref=total_v.at[:, columns(member(offset))],
            dst_ref=arrived_v.at[at],
            send_sem=part_send.at[at],
            recv_sem=part_recv.at[at],
            device_id=(sec, member(offset)),
            device_id_type=MESH,
        )
        send.start()
        sends.append(send)

    own = total_v[:, columns(ten)] + state_v[:, columns(ten)].astype(jnp.float32)
    for at in reversed(range(tensors - 1)):
        sends[at].wait_recv()
        own = own + arrived_v[at]
    result_v[...] = own.astype(jnp.bfloat16)

    def handing(at, offset, which):
        return pltpu.make_async_remote_copy(
            src_ref=result_v,
            dst_ref=handed.at[:, columns(which)],
            send_sem=res_send.at[at],
            recv_sem=res_recv.at[at],
            device_id=(after, member(offset)),
            device_id_type=MESH,
        )

    for at, offset in enumerate(offsets):
        handing(at, offset, ten).start()
    for send in sends:
        send.wait_send()
    for at, offset in enumerate(offsets):
        handing(at, offset, origin(offset)).wait_recv()
    for at, offset in enumerate(offsets):
        handing(at, offset, ten).wait_send()


def store_kernel(*refs):
    count = (len(refs) - 1) // 2
    copies = [
        pltpu.make_async_copy(refs[at], refs[count + at], refs[-1].at[at]) for at in range(count)
    ]
    for copy in copies:
        copy.start()
    for copy in copies:
        copy.wait()


def solution(mesh):
    sections, tensors = mesh.shape["section"], mesh.shape["tensor"]

    def body(state, gain_in, w_query, w_key, w_value, w_output, query_gain, key_gain, ck, cv, lengths):
        _, rows, width = state.shape
        query_width = w_query.shape[2]
        slots = ck.shape[3]
        block = width // tensors
        hbm = pl.BlockSpec(memory_space=pltpu.HBM)
        vmem = pl.BlockSpec(memory_space=pltpu.VMEM)

        def kernel(*refs):
            tick_kernel(sections, tensors, *refs)

        operands = (
            state, gain_in, w_query, w_key, w_value, w_output, query_gain, key_gain, ck, cv, lengths
        )
        operands = [pltpu.with_memory_space_constraint(x, pltpu.HBM) for x in operands]
        shapes = ((rows, width), (rows, HD), (rows, HD))
        results = pl.pallas_call(
            kernel,
            out_shape=tuple(pltpu.VMEM(shape, jnp.bfloat16) for shape in shapes),
            in_specs=[hbm] * 11,
            out_specs=(vmem, vmem, vmem),
            scratch_shapes=[
                pltpu.VMEM((rows, width), jnp.bfloat16),
                pltpu.VMEM((1, width), jnp.bfloat16),
                pltpu.VMEM((width, 2 * HD), jnp.bfloat16),
                pltpu.VMEM((GROUPS, width, query_width // GROUPS), jnp.bfloat16),
                pltpu.VMEM((GROUPS, query_width // GROUPS, width), jnp.bfloat16),
                pltpu.VMEM((1, HD), jnp.bfloat16),
                pltpu.VMEM((1, HD), jnp.bfloat16),
                pltpu.VMEM((rows, slots, HD), jnp.bfloat16),
                pltpu.VMEM((rows, slots, HD), jnp.bfloat16),
                pltpu.VMEM((1, rows), jnp.int32),
                pltpu.VMEM((rows, width), jnp.float32),
                pltpu.VMEM((tensors - 1, rows, block), jnp.float32),
                pltpu.VMEM((rows, block), jnp.bfloat16),
                pltpu.SemaphoreType.DMA((7,)),
                pltpu.SemaphoreType.DMA((2,)),
                pltpu.SemaphoreType.DMA((GROUPS,)),
                pltpu.SemaphoreType.DMA((GROUPS,)),
                pltpu.SemaphoreType.DMA((tensors - 1,)),
                pltpu.SemaphoreType.DMA((tensors - 1,)),
                pltpu.SemaphoreType.DMA((tensors,)),
                pltpu.SemaphoreType.DMA((tensors,)),
            ],
            compiler_params=pltpu.CompilerParams(
                collective_id=0, has_side_effects=True, vmem_limit_bytes=48 * 1024 * 1024
            ),
            cost_estimate=pl.CostEstimate(
                flops=4 * rows * width * (query_width + HD),
                bytes_accessed=4 * width * (query_width + HD),
                transcendentals=rows * rows * slots * 8,
            ),
            name="tick",
        )(*operands)
        handed, new_key, new_value = pl.pallas_call(
            store_kernel,
            out_shape=tuple(pltpu.HBM(shape, jnp.bfloat16) for shape in shapes),
            in_specs=[vmem] * 3,
            out_specs=(hbm, hbm, hbm),
            scratch_shapes=[pltpu.SemaphoreType.DMA((3,))],
            compiler_params=pltpu.CompilerParams(vmem_limit_bytes=8 * 1024 * 1024),
            name="store",
        )(*results)
        return (
            handed[None],
            new_key.reshape(1, rows, 1, HD),
            new_value.reshape(1, rows, 1, HD),
        )

    placed = (
        P("section", None, None),
        P("section", None),
        P("section", None, "tensor"),
        P("section", None, "tensor"),
        P("section", None, "tensor"),
        P("section", "tensor", None),
        P("section", None),
        P("section", None),
        P("section", None, "tensor", None, None),
        P("section", None, "tensor", None, None),
        P("section", None),
    )
    return jax.shard_map(
        body,
        mesh=mesh,
        in_specs=placed,
        out_specs=(
            P("section", None, None),
            P("section", None, "tensor", None),
            P("section", None, "tensor", None),
        ),
        check_vma=False,
    )
```

```python
import jax
import jax.numpy as jnp
from jax import lax
from jax.experimental import pallas as pl
from jax.experimental.pallas import tpu as pltpu
from jax.sharding import PartitionSpec as P

HD = 128
CORES = 2
CHUNKS = 5
EPSILON = 1e-06
ROPE_BASE = 1000000.0
MESH = pl.DeviceIdType.MESH


def inverse_rms(values):
    return lax.rsqrt(jnp.mean(values * values, axis=-1, keepdims=True) + EPSILON)


def tick_kernel(
    sections,
    tensors,
    state_hbm,
    gain_hbm,
    wq_hbm,
    wk_hbm,
    wv_hbm,
    wo_hbm,
    qgain_hbm,
    kgain_hbm,
    ck_hbm,
    cv_hbm,
    len_hbm,
    handed,
    nk_out,
    nv_out,
    state_v,
    gain_v,
    normed_v,
    w_v,
    total_v,
    wo_v,
    qgain_v,
    kgain_v,
    ck_v,
    cv_v,
    len_v,
    partial_v,
    arrived_v,
    result_v,
    small_sem,
    w_sem,
    wo_sem,
    part_send,
    part_recv,
    res_send,
    res_recv,
):
    rows, width = state_v.shape
    heads = wq_hbm.shape[2] // HD
    depth = width // CHUNKS
    block = width // tensors
    slots = ck_v.shape[1]

    sec = lax.axis_index("section")
    ten = lax.axis_index("tensor")
    chip, core = ten // CORES, ten % CORES
    chips = tensors // CORES
    after = (sec + 1) % sections
    before = (sec + sections - 1) % sections

    offsets = [(dy, dc) for dy in range(1, chips) for dc in range(CORES)]
    offsets += [(0, dc) for dc in range(1, CORES)] + [(0, 0)]

    def member(offset):
        return ((chip + offset[0]) % chips) * CORES + (core + offset[1]) % CORES

    def origin(offset):
        return ((chip + chips - offset[0]) % chips) * CORES + (
            core + CORES - offset[1]
        ) % CORES

    def columns(which):
        return pl.ds(pl.multiple_of(which * block, 128), block)

    small = [
        pltpu.make_async_copy(source, target, small_sem.at[at])
        for at, (source, target) in enumerate(
            [
                (state_hbm.at[0], state_v),
                (gain_hbm, gain_v),
                (len_hbm, len_v),
                (qgain_hbm, qgain_v),
                (kgain_hbm, kgain_v),
                (ck_hbm.at[0, :, 0], ck_v),
                (cv_hbm.at[0, :, 0], cv_v),
            ]
        )
    ]
    for copy in small[:5]:
        copy.start()
    query_width = heads * HD

    def weights(c):
        span = pl.ds(pl.multiple_of(c * depth, depth), depth)
        return [
            pltpu.make_async_copy(
                wq_hbm.at[0, span], w_v.at[span, pl.ds(0, query_width)], w_sem.at[c, 0]
            ),
            pltpu.make_async_copy(
                wk_hbm.at[0, span], w_v.at[span, pl.ds(query_width, HD)], w_sem.at[c, 1]
            ),
            pltpu.make_async_copy(
                wv_hbm.at[0, span], w_v.at[span, pl.ds(query_width + HD, HD)], w_sem.at[c, 2]
            ),
        ]

    for c in range(CHUNKS):
        for copy in weights(c):
            copy.start()
    for copy in small[5:]:
        copy.start()

    chip_order = [(chip + 1 + h) % chips for h in range(chips)]
    projections = [
        pltpu.make_async_copy(
            wo_hbm.at[0, :, pl.ds(pl.multiple_of(which * CORES * block, 128), CORES * block)],
            wo_v.at[h],
            wo_sem.at[h],
        )
        for h, which in enumerate(chip_order)
    ]

    barrier = pltpu.get_barrier_semaphore()
    for offset in offsets[:-1]:
        pl.semaphore_signal(
            barrier, inc=1, device_id=(sec, member(offset)), device_id_type=MESH
        )
    for offset in offsets:
        pl.semaphore_signal(
            barrier, inc=1, device_id=(before, member(offset)), device_id_type=MESH
        )

    for copy in small[:5]:
        copy.wait()
    hidden = state_v[...].astype(jnp.float32)
    normed = (hidden * inverse_rms(hidden) * gain_v[...].astype(jnp.float32)).astype(jnp.bfloat16)
    for c in range(CHUNKS):
        normed_v[c] = normed[:, c * depth : (c + 1) * depth]
    total_v[...] = jnp.zeros_like(total_v)

    on_diagonal = lax.broadcasted_iota(jnp.int32, (rows, rows), 0) == lax.broadcasted_iota(
        jnp.int32, (rows, rows), 1
    )
    spread = jnp.broadcast_to(len_v[...].astype(jnp.float32), (rows, rows))
    position = jnp.sum(jnp.where(on_diagonal, spread, 0.0), axis=1, keepdims=True)
    lane = lax.broadcasted_iota(jnp.int32, (rows, HD), 1)
    half = HD // 2
    index = jnp.where(lane < half, lane, lane - half).astype(jnp.float32)
    frequency = jnp.exp(index * (-2.0 / HD * 13.815510557964274))
    angles = position * frequency
    cosine = jnp.cos(angles)
    sine = jnp.sin(angles)
    sine = jnp.where(lane < half, -sine, sine)

    def rotate(values, cosines, sines):
        return values * cosines + pltpu.roll(values, half, 1) * sines

    gap = (
        lax.broadcasted_iota(jnp.int32, (rows, rows * slots), 1)
        - lax.broadcasted_iota(jnp.int32, (rows, rows * slots), 0) * slots
    ).astype(jnp.float32)
    excluded = jnp.where((gap >= 0.0) & (gap < position), 0.0, -1e30)

    def stacked(values):
        return jnp.concatenate([values] * heads, axis=0)

    cosine_all, sine_all, excluded_all = stacked(cosine), stacked(sine), stacked(excluded)
    query_gain = qgain_v[...].astype(jnp.float32)
    key_gain = kgain_v[...].astype(jnp.float32)

    def project(c, carry):
        for copy in weights(c):
            copy.wait()

        @pl.when(c == 1)
        def _():
            for copy in projections:
                copy.start()

        span = pl.ds(pl.multiple_of(c * depth, depth), depth)
        total_v[...] += jnp.dot(normed_v[c], w_v[span, :], preferred_element_type=jnp.float32)
        return carry

    lax.fori_loop(0, CHUNKS, project, 0)
    total = total_v[...]

    key_raw = total[:, query_width : query_width + HD]
    new_value = total[:, query_width + HD :].astype(jnp.bfloat16)
    new_key = rotate(key_raw * inverse_rms(key_raw) * key_gain, cosine, sine).astype(jnp.bfloat16)
    nk_out[...] = new_key
    nv_out[...] = new_value

    query = jnp.concatenate([total[:, h * HD : (h + 1) * HD] for h in range(heads)], axis=0)
    query_rot = rotate(query * inverse_rms(query) * query_gain, cosine_all, sine_all).astype(
        jnp.bfloat16
    )

    scale = HD**-0.5
    own_score = (
        jnp.sum(
            query_rot.astype(jnp.float32) * stacked(new_key.astype(jnp.float32)),
            axis=1,
            keepdims=True,
        )
        * scale
    )
    small[5].wait()
    keys = ck_v[...].reshape(rows * slots, HD)
    scores = (
        lax.dot_general(
            query_rot, keys, (((1,), (1,)), ((), ())), preferred_element_type=jnp.float32
        )
        * scale
        + excluded_all
    )
    row_max = jnp.maximum(jnp.max(scores, axis=1, keepdims=True), own_score)
    cache_exp = jnp.exp(scores - row_max)
    own_exp = jnp.exp(own_score - row_max)
    share = 1.0 / (jnp.sum(cache_exp, axis=1, keepdims=True) + own_exp)
    cache_prob = (cache_exp * share).astype(jnp.bfloat16)
    own_prob = (own_exp * share).astype(jnp.bfloat16).astype(jnp.float32)
    small[6].wait()
    attended = jnp.dot(
        cache_prob, cv_v[...].reshape(rows * slots, HD), preferred_element_type=jnp.float32
    )
    attended = (attended + own_prob * stacked(new_value.astype(jnp.float32))).astype(jnp.bfloat16)
    attended = jnp.concatenate(
        [attended[h * rows : (h + 1) * rows] for h in range(heads)], axis=1
    )

    pl.semaphore_wait(barrier, 2 * tensors - 1)

    def sending(h, source, target, which):
        return pltpu.make_async_remote_copy(
            src_ref=partial_v.at[h, source],
            dst_ref=arrived_v.at[h, target],
            send_sem=part_send.at[h, source],
            recv_sem=part_recv.at[h, target],
            device_id=(sec, which),
            device_id_type=MESH,
        )

    sends = []
    other = (core + 1) % CORES
    for h, which in enumerate(chip_order):
        projections[h].wait()
        partial = jnp.dot(attended, wo_v[h], preferred_element_type=jnp.float32)
        for c in range(CORES):
            partial_v[h, c] = partial[:, c * block : (c + 1) * block]
        if h < chips - 1:
            sends += [sending(h, c, core, which * CORES + c) for c in range(CORES)]
        else:
            sends += [sending(h, other, core, chip * CORES + other)]
        for send in sends[-CORES if h < chips - 1 else -1 :]:
            send.start()

    own = partial_v[chips - 1, core] + state_v[:, columns(ten)].astype(jnp.float32)
    sending(chips - 1, core, other, chip * CORES + other).wait_recv()
    own = own + arrived_v[chips - 1, other]
    for h in range(chips - 1):
        for c in range(CORES):
            sending(h, c, c, chip_order[h] * CORES + c).wait_recv()
            own = own + arrived_v[h, c]
    result_v[...] = own.astype(jnp.bfloat16)

    def handing(at, offset, which):
        return pltpu.make_async_remote_copy(
            src_ref=result_v,
            dst_ref=handed.at[:, columns(which)],
            send_sem=res_send.at[at],
            recv_sem=res_recv.at[at],
            device_id=(after, member(offset)),
            device_id_type=MESH,
        )

    for at, offset in enumerate(offsets):
        handing(at, offset, ten).start()
    for send in sends:
        send.wait_send()
    for at, offset in enumerate(offsets):
        handing(at, offset, origin(offset)).wait_recv()
    for at, offset in enumerate(offsets):
        handing(at, offset, ten).wait_send()


def store_kernel(*refs):
    count = (len(refs) - 1) // 2
    copies = [
        pltpu.make_async_copy(refs[at], refs[count + at], refs[-1].at[at]) for at in range(count)
    ]
    for copy in copies:
        copy.start()
    for copy in copies:
        copy.wait()


def solution(mesh):
    sections, tensors = mesh.shape["section"], mesh.shape["tensor"]

    def body(state, gain_in, w_query, w_key, w_value, w_output, query_gain, key_gain, ck, cv, lengths):
        _, rows, width = state.shape
        query_width = w_query.shape[2]
        slots = ck.shape[3]
        block = width // tensors
        chips = tensors // CORES
        hbm = pl.BlockSpec(memory_space=pltpu.HBM)
        vmem = pl.BlockSpec(memory_space=pltpu.VMEM)

        def kernel(*refs):
            tick_kernel(sections, tensors, *refs)

        operands = (
            state, gain_in, w_query, w_key, w_value, w_output, query_gain, key_gain, ck, cv, lengths
        )
        operands = [pltpu.with_memory_space_constraint(x, pltpu.HBM) for x in operands]
        shapes = ((rows, width), (rows, HD), (rows, HD))
        results = pl.pallas_call(
            kernel,
            out_shape=tuple(pltpu.VMEM(shape, jnp.bfloat16) for shape in shapes),
            in_specs=[hbm] * 11,
            out_specs=(vmem, vmem, vmem),
            scratch_shapes=[
                pltpu.VMEM((rows, width), jnp.bfloat16),
                pltpu.VMEM((1, width), jnp.bfloat16),
                pltpu.VMEM((CHUNKS, rows, width // CHUNKS), jnp.bfloat16),
                pltpu.VMEM((width, query_width + 2 * HD), jnp.bfloat16),
                pltpu.VMEM((rows, query_width + 2 * HD), jnp.float32),
                pltpu.VMEM((chips, query_width, CORES * block), jnp.bfloat16),
                pltpu.VMEM((1, HD), jnp.bfloat16),
                pltpu.VMEM((1, HD), jnp.bfloat16),
                pltpu.VMEM((rows, slots, HD), jnp.bfloat16),
                pltpu.VMEM((rows, slots, HD), jnp.bfloat16),
                pltpu.VMEM((1, rows), jnp.int32),
                pltpu.VMEM((chips, CORES, rows, block), jnp.float32),
                pltpu.VMEM((chips, CORES, rows, block), jnp.float32),
                pltpu.VMEM((rows, block), jnp.bfloat16),
                pltpu.SemaphoreType.DMA((7,)),
                pltpu.SemaphoreType.DMA((CHUNKS, 3)),
                pltpu.SemaphoreType.DMA((chips,)),
                pltpu.SemaphoreType.DMA((chips, CORES)),
                pltpu.SemaphoreType.DMA((chips, CORES)),
                pltpu.SemaphoreType.DMA((tensors,)),
                pltpu.SemaphoreType.DMA((tensors,)),
            ],
            compiler_params=pltpu.CompilerParams(
                collective_id=0, has_side_effects=True, vmem_limit_bytes=48 * 1024 * 1024
            ),
            cost_estimate=pl.CostEstimate(
                flops=4 * rows * width * (query_width + HD),
                bytes_accessed=4 * width * (query_width + HD),
                transcendentals=rows * rows * slots * 8,
            ),
            name="tick",
        )(*operands)
        handed, new_key, new_value = pl.pallas_call(
            store_kernel,
            out_shape=tuple(pltpu.HBM(shape, jnp.bfloat16) for shape in shapes),
            in_specs=[vmem] * 3,
            out_specs=(hbm, hbm, hbm),
            scratch_shapes=[pltpu.SemaphoreType.DMA((3,))],
            compiler_params=pltpu.CompilerParams(vmem_limit_bytes=8 * 1024 * 1024),
            name="store",
        )(*results)
        return (
            handed[None],
            new_key.reshape(1, rows, 1, HD),
            new_value.reshape(1, rows, 1, HD),
        )

    placed = (
        P("section", None, None),
        P("section", None),
        P("section", None, "tensor"),
        P("section", None, "tensor"),
        P("section", None, "tensor"),
        P("section", "tensor", None),
        P("section", None),
        P("section", None),
        P("section", None, "tensor", None, None),
        P("section", None, "tensor", None, None),
        P("section", None),
    )
    return jax.shard_map(
        body,
        mesh=mesh,
        in_specs=placed,
        out_specs=(
            P("section", None, None),
            P("section", None, "tensor", None),
            P("section", None, "tensor", None),
        ),
        check_vma=False,
    )
```

```python
import jax
import jax.numpy as jnp
from jax import lax
from jax.experimental import pallas as pl
from jax.experimental.pallas import tpu as pltpu
from jax.sharding import PartitionSpec as P

HD = 128
CORES = 2
CHUNKS = 5
EPSILON = 1e-06
ROPE_BASE = 1000000.0
MESH = pl.DeviceIdType.MESH


def inverse_rms(values):
    return lax.rsqrt(jnp.mean(values * values, axis=-1, keepdims=True) + EPSILON)


def tick_kernel(
    sections,
    tensors,
    state_hbm,
    gain_hbm,
    wq_hbm,
    wk_hbm,
    wv_hbm,
    wo_hbm,
    qgain_hbm,
    kgain_hbm,
    ck_hbm,
    cv_hbm,
    len_hbm,
    handed,
    nk_out,
    nv_out,
    state_v,
    gain_v,
    w_v,
    wo_v,
    qgain_v,
    kgain_v,
    ck_v,
    cv_v,
    len_v,
    partial_v,
    arrived_v,
    result_v,
    small_sem,
    w_sem,
    wo_sem,
    part_send,
    part_recv,
    res_send,
    res_recv,
):
    rows, width = state_v.shape
    heads = wq_hbm.shape[2] // HD
    depth = width // CHUNKS
    block = width // tensors
    slots = ck_v.shape[1]

    sec = lax.axis_index("section")
    ten = lax.axis_index("tensor")
    chip, core = ten // CORES, ten % CORES
    chips = tensors // CORES
    after = (sec + 1) % sections
    before = (sec + sections - 1) % sections

    offsets = [(dy, dc) for dy in range(1, chips) for dc in range(CORES)]
    offsets += [(0, dc) for dc in range(1, CORES)] + [(0, 0)]

    def member(offset):
        return ((chip + offset[0]) % chips) * CORES + (core + offset[1]) % CORES

    def origin(offset):
        return ((chip + chips - offset[0]) % chips) * CORES + (
            core + CORES - offset[1]
        ) % CORES

    def columns(which):
        return pl.ds(pl.multiple_of(which * block, 128), block)

    small = [
        pltpu.make_async_copy(source, target, small_sem.at[at])
        for at, (source, target) in enumerate(
            [
                (state_hbm.at[0], state_v),
                (gain_hbm, gain_v),
                (len_hbm, len_v),
                (qgain_hbm, qgain_v),
                (kgain_hbm, kgain_v),
                (ck_hbm.at[0, :, 0], ck_v),
                (cv_hbm.at[0, :, 0], cv_v),
            ]
        )
    ]
    for copy in small[:5]:
        copy.start()
    query_width = heads * HD

    def weights(c):
        span = pl.ds(pl.multiple_of(c * depth, depth), depth)
        return [
            pltpu.make_async_copy(
                wq_hbm.at[0, span], w_v.at[span, pl.ds(0, query_width)], w_sem.at[c, 0]
            ),
            pltpu.make_async_copy(
                wk_hbm.at[0, span], w_v.at[span, pl.ds(query_width, HD)], w_sem.at[c, 1]
            ),
            pltpu.make_async_copy(
                wv_hbm.at[0, span], w_v.at[span, pl.ds(query_width + HD, HD)], w_sem.at[c, 2]
            ),
        ]

    for c in range(CHUNKS):
        for copy in weights(c):
            copy.start()
    for copy in small[5:]:
        copy.start()

    chip_order = [(chip + 1 + h) % chips for h in range(chips)]
    projections = [
        pltpu.make_async_copy(
            wo_hbm.at[0, :, pl.ds(pl.multiple_of(which * CORES * block, 128), CORES * block)],
            wo_v.at[h],
            wo_sem.at[h],
        )
        for h, which in enumerate(chip_order)
    ]

    for copy in projections:
        copy.start()

    barrier = pltpu.get_barrier_semaphore()
    for offset in offsets[:-1]:
        pl.semaphore_signal(
            barrier, inc=1, device_id=(sec, member(offset)), device_id_type=MESH
        )
    for offset in offsets:
        pl.semaphore_signal(
            barrier, inc=1, device_id=(before, member(offset)), device_id_type=MESH
        )

    lines = (slots // 8 + 1) * 8
    lane = lax.broadcasted_iota(jnp.int32, (lines, HD), 1)
    half = HD // 2
    index = jnp.where(lane < half, lane, lane - half).astype(jnp.float32)
    frequency = jnp.exp(index * (-2.0 / HD * 13.815510557964274))
    angles = lax.broadcasted_iota(jnp.int32, (lines, HD), 0).astype(jnp.float32) * frequency
    unused = jnp.zeros((HD - lines, HD), jnp.float32)
    sine_table = jnp.sin(angles)
    sine_table = jnp.where(lane < half, -sine_table, sine_table)
    cosine_table = jnp.concatenate([jnp.cos(angles), unused], axis=0)
    sine_table = jnp.concatenate([sine_table, unused], axis=0)

    for copy in small[:5]:
        copy.wait()
    hidden = state_v[...].astype(jnp.float32)
    normed = (hidden * inverse_rms(hidden) * gain_v[...].astype(jnp.float32)).astype(jnp.bfloat16)

    on_diagonal = lax.broadcasted_iota(jnp.int32, (rows, rows), 0) == lax.broadcasted_iota(
        jnp.int32, (rows, rows), 1
    )
    spread = jnp.broadcast_to(len_v[...].astype(jnp.float32), (rows, rows))
    position = jnp.sum(jnp.where(on_diagonal, spread, 0.0), axis=1, keepdims=True)
    chosen = (lax.broadcasted_iota(jnp.int32, (rows, HD), 1).astype(jnp.float32) == position).astype(
        jnp.float32
    )

    def picked(table):
        return jnp.dot(
            chosen, table, precision=lax.Precision.HIGHEST, preferred_element_type=jnp.float32
        )

    cosine, sine = picked(cosine_table), picked(sine_table)

    def rotate(values, cosines, sines):
        return values * cosines + pltpu.roll(values, half, 1) * sines

    gap = (
        lax.broadcasted_iota(jnp.int32, (rows, rows * slots), 1)
        - lax.broadcasted_iota(jnp.int32, (rows, rows * slots), 0) * slots
    ).astype(jnp.float32)
    excluded = jnp.where((gap >= 0.0) & (gap < position), 0.0, -1e30)

    def stacked(values):
        return jnp.concatenate([values] * heads, axis=0)

    cosine_all, sine_all, excluded_all = stacked(cosine), stacked(sine), stacked(excluded)
    query_gain = qgain_v[...].astype(jnp.float32)
    key_gain = kgain_v[...].astype(jnp.float32)

    total = None
    for c in range(CHUNKS):
        for copy in weights(c):
            copy.wait()
        term = jnp.dot(
            normed[:, c * depth : (c + 1) * depth],
            w_v[c * depth : (c + 1) * depth, :],
            preferred_element_type=jnp.float32,
        )
        total = term if total is None else total + term

    key_raw = total[:, query_width : query_width + HD]
    new_value = total[:, query_width + HD :].astype(jnp.bfloat16)
    new_key = rotate(key_raw * inverse_rms(key_raw) * key_gain, cosine, sine).astype(jnp.bfloat16)
    nk_out[...] = new_key
    nv_out[...] = new_value

    query = jnp.concatenate([total[:, h * HD : (h + 1) * HD] for h in range(heads)], axis=0)
    query_rot = rotate(query * inverse_rms(query) * query_gain, cosine_all, sine_all).astype(
        jnp.bfloat16
    )

    scale = HD**-0.5
    own_score = (
        jnp.sum(
            query_rot.astype(jnp.float32) * stacked(new_key.astype(jnp.float32)),
            axis=1,
            keepdims=True,
        )
        * scale
    )
    small[5].wait()
    keys = ck_v[...].reshape(rows * slots, HD)
    scores = (
        lax.dot_general(
            query_rot, keys, (((1,), (1,)), ((), ())), preferred_element_type=jnp.float32
        )
        * scale
        + excluded_all
    )
    row_max = jnp.maximum(jnp.max(scores, axis=1, keepdims=True), own_score)
    cache_exp = jnp.exp(scores - row_max)
    own_exp = jnp.exp(own_score - row_max)
    share = 1.0 / (jnp.sum(cache_exp, axis=1, keepdims=True) + own_exp)
    cache_prob = (cache_exp * share).astype(jnp.bfloat16)
    own_prob = (own_exp * share).astype(jnp.bfloat16).astype(jnp.float32)
    small[6].wait()
    attended = jnp.dot(
        cache_prob, cv_v[...].reshape(rows * slots, HD), preferred_element_type=jnp.float32
    )
    attended = (attended + own_prob * stacked(new_value.astype(jnp.float32))).astype(jnp.bfloat16)
    attended = jnp.concatenate(
        [attended[h * rows : (h + 1) * rows] for h in range(heads)], axis=1
    )

    pl.semaphore_wait(barrier, 2 * tensors - 1)

    def sending(h, source, target, which):
        return pltpu.make_async_remote_copy(
            src_ref=partial_v.at[h, source],
            dst_ref=arrived_v.at[h, target],
            send_sem=part_send.at[h, source],
            recv_sem=part_recv.at[h, target],
            device_id=(sec, which),
            device_id_type=MESH,
        )

    sends = []
    other = (core + 1) % CORES
    for h, which in enumerate(chip_order):
        projections[h].wait()
        partial = jnp.dot(attended, wo_v[h], preferred_element_type=jnp.float32)
        for c in range(CORES):
            partial_v[h, c] = partial[:, c * block : (c + 1) * block]
        if h < chips - 1:
            sends += [sending(h, c, core, which * CORES + c) for c in range(CORES)]
        else:
            sends += [sending(h, other, core, chip * CORES + other)]
        for send in sends[-CORES if h < chips - 1 else -1 :]:
            send.start()

    own = partial_v[chips - 1, core] + state_v[:, columns(ten)].astype(jnp.float32)
    sending(chips - 1, core, other, chip * CORES + other).wait_recv()
    own = own + arrived_v[chips - 1, other]
    for h in range(chips - 1):
        for c in range(CORES):
            sending(h, c, c, chip_order[h] * CORES + c).wait_recv()
            own = own + arrived_v[h, c]
    result_v[...] = own.astype(jnp.bfloat16)

    def handing(at, offset, which):
        return pltpu.make_async_remote_copy(
            src_ref=result_v,
            dst_ref=handed.at[:, columns(which)],
            send_sem=res_send.at[at],
            recv_sem=res_recv.at[at],
            device_id=(after, member(offset)),
            device_id_type=MESH,
        )

    for at, offset in enumerate(offsets):
        handing(at, offset, ten).start()
    for send in sends:
        send.wait_send()
    for at, offset in enumerate(offsets):
        handing(at, offset, origin(offset)).wait_recv()
    for at, offset in enumerate(offsets):
        handing(at, offset, ten).wait_send()


def store_kernel(*refs):
    count = (len(refs) - 1) // 2
    copies = [
        pltpu.make_async_copy(refs[at], refs[count + at], refs[-1].at[at]) for at in range(count)
    ]
    for copy in copies:
        copy.start()
    for copy in copies:
        copy.wait()


def solution(mesh):
    sections, tensors = mesh.shape["section"], mesh.shape["tensor"]

    def body(state, gain_in, w_query, w_key, w_value, w_output, query_gain, key_gain, ck, cv, lengths):
        _, rows, width = state.shape
        query_width = w_query.shape[2]
        slots = ck.shape[3]
        block = width // tensors
        chips = tensors // CORES
        hbm = pl.BlockSpec(memory_space=pltpu.HBM)
        vmem = pl.BlockSpec(memory_space=pltpu.VMEM)

        def kernel(*refs):
            tick_kernel(sections, tensors, *refs)

        operands = (
            state, gain_in, w_query, w_key, w_value, w_output, query_gain, key_gain, ck, cv, lengths
        )
        operands = [pltpu.with_memory_space_constraint(x, pltpu.HBM) for x in operands]
        shapes = ((rows, width), (rows, HD), (rows, HD))
        results = pl.pallas_call(
            kernel,
            out_shape=tuple(pltpu.VMEM(shape, jnp.bfloat16) for shape in shapes),
            in_specs=[hbm] * 11,
            out_specs=(vmem, vmem, vmem),
            scratch_shapes=[
                pltpu.VMEM((rows, width), jnp.bfloat16),
                pltpu.VMEM((1, width), jnp.bfloat16),
                pltpu.VMEM((width, query_width + 2 * HD), jnp.bfloat16),
                pltpu.VMEM((chips, query_width, CORES * block), jnp.bfloat16),
                pltpu.VMEM((1, HD), jnp.bfloat16),
                pltpu.VMEM((1, HD), jnp.bfloat16),
                pltpu.VMEM((rows, slots, HD), jnp.bfloat16),
                pltpu.VMEM((rows, slots, HD), jnp.bfloat16),
                pltpu.VMEM((1, rows), jnp.int32),
                pltpu.VMEM((chips, CORES, rows, block), jnp.float32),
                pltpu.VMEM((chips, CORES, rows, block), jnp.float32),
                pltpu.VMEM((rows, block), jnp.bfloat16),
                pltpu.SemaphoreType.DMA((7,)),
                pltpu.SemaphoreType.DMA((CHUNKS, 3)),
                pltpu.SemaphoreType.DMA((chips,)),
                pltpu.SemaphoreType.DMA((chips, CORES)),
                pltpu.SemaphoreType.DMA((chips, CORES)),
                pltpu.SemaphoreType.DMA((tensors,)),
                pltpu.SemaphoreType.DMA((tensors,)),
            ],
            compiler_params=pltpu.CompilerParams(
                collective_id=0, has_side_effects=True, vmem_limit_bytes=48 * 1024 * 1024
            ),
            cost_estimate=pl.CostEstimate(
                flops=4 * rows * width * (query_width + HD),
                bytes_accessed=4 * width * (query_width + HD),
                transcendentals=rows * rows * slots * 8,
            ),
            name="tick",
        )(*operands)
        handed, new_key, new_value = pl.pallas_call(
            store_kernel,
            out_shape=tuple(pltpu.HBM(shape, jnp.bfloat16) for shape in shapes),
            in_specs=[vmem] * 3,
            out_specs=(hbm, hbm, hbm),
            scratch_shapes=[pltpu.SemaphoreType.DMA((3,))],
            compiler_params=pltpu.CompilerParams(vmem_limit_bytes=8 * 1024 * 1024),
            name="store",
        )(*results)
        return (
            handed[None],
            new_key.reshape(1, rows, 1, HD),
            new_value.reshape(1, rows, 1, HD),
        )

    placed = (
        P("section", None, None),
        P("section", None),
        P("section", None, "tensor"),
        P("section", None, "tensor"),
        P("section", None, "tensor"),
        P("section", "tensor", None),
        P("section", None),
        P("section", None),
        P("section", None, "tensor", None, None),
        P("section", None, "tensor", None, None),
        P("section", None),
    )
    return jax.shard_map(
        body,
        mesh=mesh,
        in_specs=placed,
        out_specs=(
            P("section", None, None),
            P("section", None, "tensor", None),
            P("section", None, "tensor", None),
        ),
        check_vma=False,
    )
```
